32 devices in a mesh: dp: 8 (over y, x, core), tensor: 4 (over z).
Axes of the slice: x: 2, y: 2, z: 4, core: 2. Of those that a mesh axis runs over, the one named last changes fastest.
Arguments:
- hidden: bfloat16 [4096, 4096], P('dp', 'tensor')
- w_query: bfloat16 [4096, 4096], P(None, 'tensor')
- w_key: bfloat16 [4096, 1024], P(None, 'tensor')
- w_value: bfloat16 [4096, 1024], P(None, 'tensor'), may hold values from -0.09375 to 0.09375
- w_out: bfloat16 [4096, 4096], P('tensor'), may hold values from -0.09375 to 0.09375
- doc_ids: int32 [4096], P('dp'), may hold values from 0 to 4095, as said below
- send_counts: int32 [8, 8], replicated, may hold values from 0 to 16, as said below
Outputs:
- attended: bfloat16 [5120, 4096], P('dp', 'tensor')
The draws below stay inside these ranges and needn't reach their ends.
Inputs may be any that keep to these rules, and one draw needn't show every extreme that they name: `send_counts`: the diagonal is zero and each row sums to less than 512. On index i of dp the rows that stay come first, then the rows for each destination j in increasing order of j, each such block one whole document. `doc_ids`: the rows of one document lie together on one index of dp and share one id; different documents have different ids.
All inputs are finite; a program needn't handle non-finite values.
Results may differ from the reference program's by a relative error of at most 0.014.
Values may be sent and summed in bfloat16 or wider, within the bound.
A program may use at most 128 MiB of HBM per device.

```python
import jax
import jax.numpy as jnp
from jax import lax

D = 4096
HEADS = 32
KV = 8
HD = 128
TOK_DEV = 512
SLOT = 16
TOKENS = 4096
BUF = 640
OUT_ROWS = 5120
N_DP = 8
N_TENSOR = 4


def move_plan(key):
    count_key = jax.random.fold_in(key, 11)
    coin_key = jax.random.fold_in(key, 12)
    heavy_key = jax.random.fold_in(key, 13)
    counts = jax.random.randint(count_key, (N_DP, N_DP), 0, SLOT + 1).astype(jnp.int32)
    heavy = jax.random.randint(heavy_key, (), 0, N_DP).astype(jnp.int32)
    row_index = jnp.arange(N_DP, dtype=jnp.int32)[:, None]
    col_index = jnp.arange(N_DP, dtype=jnp.int32)[None, :]
    counts = jnp.where(col_index == heavy, SLOT, counts)
    counts = jnp.where(row_index == heavy, 0, counts)
    counts = jnp.where(row_index == col_index, 0, counts)
    counts = jnp.where(col_index == (row_index + 1) % N_DP, SLOT, counts).astype(jnp.int32)
    home_len = TOK_DEV - jnp.sum(counts, axis=1)
    starts = home_len[:, None] + jnp.cumsum(counts, axis=1) - counts
    positions = jnp.arange(TOK_DEV, dtype=jnp.int32)[None, :]
    coins = jax.random.randint(coin_key, (N_DP, TOK_DEV), 0, 64)
    home_flag = (positions < home_len[:, None]) & ((coins == 0) | (positions == 0))
    block_flag = jnp.any((positions[:, :, None] == starts[:, None, :]) & (counts[:, None, :] > 0), axis=2)
    flags = home_flag | block_flag
    end_flag = jnp.concatenate([flags[:, 1:], jnp.ones((N_DP, 1), dtype=bool)], axis=1)
    positions_full = jnp.broadcast_to(positions, (N_DP, TOK_DEV))
    last = lax.cummin(jnp.where(end_flag, positions_full, TOK_DEV), axis=1, reverse=True)
    ids = jnp.arange(N_DP, dtype=jnp.int32)[:, None] * TOK_DEV + last
    return (counts, ids.reshape(-1).astype(jnp.int32))


def draw_send_counts(key, part):
    return move_plan(key)[0]


def draw_doc_ids(key, part):
    return move_plan(key)[1]


def query_base(key):
    return jax.random.normal(jax.random.fold_in(key, 21), (D, HEADS * HD), jnp.float32) * D ** (-0.5)


def draw_w_query(key, part):
    return query_base(key).astype(jnp.bfloat16)


def draw_w_key(key, part):
    fresh = jax.random.normal(jax.random.fold_in(key, 22), (D, KV * HD), jnp.float32) * D ** (-0.5)
    return fresh.astype(jnp.bfloat16)


def draw_hidden(key, part):
    values = jnp.clip(jax.random.normal(jax.random.fold_in(key, 31), (TOKENS, D), jnp.float32), -6.0, 6.0)
    return values.astype(jnp.bfloat16)


def block_levels(stream_key, dims, split, least, largest):
    level, own = 1.0, jax.random.fold_in(stream_key, 6)
    for axis_at, shards_of in split:
        heights = jnp.exp(jax.random.uniform(jax.random.fold_in(own, axis_at), (shards_of,), jnp.float32, least / len(split), largest / len(split)))
        level = level * jnp.repeat(heights, dims[axis_at] // shards_of).reshape([-1 if axis == axis_at else 1 for axis in range(len(dims))])
    return level


def gaussian(own_key, dims, width, limit, shards=(), held_as=jnp.bfloat16):
    level = block_levels(own_key, dims, shards, -0.22, 0.18) if shards else 1.0
    entries = jax.random.normal(own_key, dims, jnp.float32) * width * level
    return jnp.minimum(jnp.maximum(entries, -limit), limit).astype(held_as)


def setup_inputs(seed: int = 0) -> dict:
    splits = jax.random.split(jax.random.key(seed), 8)
    return {
        "hidden": draw_hidden(jax.random.fold_in(splits[7], 71), 0),
        "w_query": draw_w_query(jax.random.fold_in(splits[7], 71), 0),
        "w_key": draw_w_key(jax.random.fold_in(splits[7], 71), 0),
        "w_value": gaussian(splits[3], (D, KV * HD), D ** -0.5, 0.09375, ((1, 4),)),
        "w_out": gaussian(splits[4], (HEADS * HD, D), (HEADS * HD) ** -0.5, 0.09375, ((0, 4),)),
        "doc_ids": draw_doc_ids(jax.random.fold_in(splits[7], 71), 0),
        "send_counts": draw_send_counts(jax.random.fold_in(splits[7], 71), 0),
    }


def reference(hidden, w_query, w_key, w_value, w_out, doc_ids, send_counts):
    all_query = jnp.dot(hidden, w_query, preferred_element_type=jnp.float32).astype(jnp.bfloat16)
    all_key = jnp.dot(hidden, w_key, preferred_element_type=jnp.float32).astype(jnp.bfloat16)
    all_value = jnp.dot(hidden, w_value, preferred_element_type=jnp.float32).astype(jnp.bfloat16)
    home_len = TOK_DEV - jnp.sum(send_counts, axis=1)
    block_start = home_len[:, None] + jnp.cumsum(send_counts, axis=1) - send_counts
    slot_ids = jnp.arange(SLOT, dtype=jnp.int32)
    peer_ids = jnp.arange(N_DP, dtype=jnp.int32)
    out_weight = w_out.astype(jnp.float32).reshape(N_TENSOR, (HEADS * HD) // N_TENSOR, D)
    group = HEADS // KV

    def one_buffer(target):
        incoming = send_counts[:, target]
        starts = block_start[:, target]
        home_rows = (target * TOK_DEV + jnp.arange(TOK_DEV, dtype=jnp.int32)).astype(jnp.int32)
        local_rows = jnp.minimum(starts[:, None] + slot_ids[None, :], TOK_DEV - 1)
        recv_rows = (peer_ids[:, None] * TOK_DEV + local_rows).astype(jnp.int32)
        recv_valid = slot_ids[None, :] < incoming[:, None]
        index = jnp.concatenate([home_rows, recv_rows.reshape(-1)]).astype(jnp.int32)
        recv_labels = jnp.where(recv_valid, -1 - peer_ids[:, None], -1 - N_DP - peer_ids[:, None] * SLOT - slot_ids[None, :])
        labels = jnp.concatenate([doc_ids[home_rows], recv_labels.reshape(-1).astype(jnp.int32)])
        valid = jnp.concatenate([jnp.arange(TOK_DEV) < home_len[target], recv_valid.reshape(-1)])
        queries = all_query[index].astype(jnp.float32).reshape(BUF, KV, group, HD)
        key_rows = all_key[index].astype(jnp.float32).reshape(BUF, KV, HD)
        value_rows = all_value[index].astype(jnp.float32).reshape(BUF, KV, HD)
        positions = jnp.arange(BUF)
        allowed = (labels[:, None] == labels[None, :]) & (positions[None, :] <= positions[:, None])
        scores = jnp.einsum("qhgd,khd->hgqk", queries, key_rows) * (HD ** -0.5)
        scores = jnp.where(allowed[None, None], scores, -jnp.inf)
        top = jnp.max(scores, axis=-1, keepdims=True)
        expo = jnp.exp(scores - top)
        total = jnp.sum(expo, axis=-1)
        weights = lax.optimization_barrier(expo.astype(jnp.bfloat16)).astype(jnp.float32)
        mixed = jnp.einsum("hgqk,khd->qhgd", weights, value_rows) / jnp.transpose(total, (2, 0, 1))[..., None]
        mixed = lax.optimization_barrier(mixed.reshape(BUF, HEADS * HD).astype(jnp.bfloat16)).astype(jnp.float32)
        partial_sum = jnp.einsum("btc,tcd->tbd", mixed.reshape(BUF, N_TENSOR, -1), out_weight)
        partial_sum = jnp.where(valid[None, :, None], partial_sum, 0.0)
        rounded = lax.optimization_barrier(partial_sum.astype(jnp.bfloat16)).astype(jnp.float32)
        return jnp.sum(rounded, axis=0).astype(jnp.bfloat16)

    result = lax.map(one_buffer, jnp.arange(N_DP, dtype=jnp.int32))
    return result.reshape(OUT_ROWS, D)
```

```python
import functools

import jax
import jax.numpy as jnp
from jax import lax
from jax.experimental import pallas as pl
from jax.experimental.pallas import tpu as pltpu
from jax.sharding import PartitionSpec as P

HD = 128
SLOT = 16
TILE = 256
CHUNKS = 4
MESH = pl.DeviceIdType.MESH
F32 = jnp.float32
BF16 = jnp.bfloat16


def layer_kernel(
    peers, parts, chunks, q_heads, kv_heads,
    hidden_ref, wq_ref, wk_ref, wv_ref, wo_ref, docs_ref, counts_ref,
    out_ref,
    wqkv, wout, hid, heads, mixed, partial, arrived, acc, final, outgoing, slots, doc_col,
    load_sem, ag_send, ag_recv, rs_send, rs_recv, mv_send, mv_recv,
):
    rows_all, width = hidden_ref.shape
    count = rows_all // chunks
    group = q_heads // kv_heads
    me = lax.axis_index("dp")
    z = lax.axis_index("tensor")
    tiles_per_block = width // TILE

    def inside(position):
        return (position >= 0) & (position < parts)

    def clamp(position):
        return jnp.minimum(jnp.maximum(position, 0), parts - 1)

    q_cols, kv_cols = q_heads * HD, kv_heads * HD
    load_own = pltpu.make_async_copy(hidden_ref, hid.at[z], load_sem.at[0])
    loads_qkv = [
        pltpu.make_async_copy(wq_ref, wqkv.at[:, pl.ds(0, q_cols)], load_sem.at[1]),
        pltpu.make_async_copy(wk_ref, wqkv.at[:, pl.ds(q_cols, kv_cols)], load_sem.at[2]),
        pltpu.make_async_copy(wv_ref, wqkv.at[:, pl.ds(q_cols + kv_cols, kv_cols)], load_sem.at[3]),
    ]
    load_out = pltpu.make_async_copy(wo_ref, wout, load_sem.at[4])

    barrier = pltpu.get_barrier_semaphore()
    for step in (-1, 1):
        @pl.when(inside(z + step))
        def _(step=step):
            pl.semaphore_signal(barrier, inc=1, device_id={"tensor": z + step}, device_id_type=MESH)

    @pl.loop(1, peers)
    def _(i):
        pl.semaphore_signal(barrier, inc=1, device_id={"dp": lax.rem(me + i, peers)}, device_id_type=MESH)

    load_own.start()
    for load in loads_qkv:
        load.start()
    load_out.start()
    neighbours = inside(z - 1).astype(jnp.int32) + inside(z + 1).astype(jnp.int32)
    pl.semaphore_wait(barrier, peers - 1 + neighbours)

    def rows_of(c):
        return pl.ds(c * count, count)

    def gather_copy(way, c, hop):
        step = 1 - 2 * way
        owner = clamp(z - step * (hop - 1))
        block = hid.at[owner, rows_of(c), :]
        return pltpu.make_async_remote_copy(
            src_ref=hidden_ref.at[rows_of(c), :] if hop == 1 else block,
            dst_ref=block,
            send_sem=ag_send.at[way, c, hop - 1],
            recv_sem=ag_recv.at[way, c, hop - 1],
            device_id={"tensor": clamp(z + step)},
            device_id_type=MESH,
        )

    def gather_sends(way, hop):
        step = 1 - 2 * way
        return inside(z - step * (hop - 1)) & inside(z + step)

    def gather_start(c, hop):
        for way in (0, 1):
            @pl.when(gather_sends(way, hop))
            def _(way=way):
                gather_copy(way, c, hop).start()

    def gather_take(c, hop):
        for way in (0, 1):
            step = 1 - 2 * way

            @pl.when(inside(z - step * hop))
            def _(way=way, step=step):
                block = hid.at[clamp(z - step * hop), rows_of(c), :]
                pltpu.make_async_remote_copy(
                    src_ref=block,
                    dst_ref=block,
                    send_sem=ag_send.at[way, c, hop - 1],
                    recv_sem=ag_recv.at[way, c, hop - 1],
                    device_id={"tensor": clamp(z + step)},
                    device_id_type=MESH,
                ).wait_recv()
        if hop < parts - 1:
            gather_start(c, hop + 1)

    def sum_copy(way, c, hop, source):
        step = 1 - 2 * way
        return pltpu.make_async_remote_copy(
            src_ref=source,
            dst_ref=arrived.at[way, c, hop - 1],
            send_sem=rs_send.at[way, c, hop - 1],
            recv_sem=rs_recv.at[way, c, hop - 1],
            device_id={"tensor": clamp(z + step)},
            device_id_type=MESH,
        )

    def sum_hop(c, hop):
        for way in (0, 1):
            step = 1 - 2 * way
            block = z + step * (parts - hop)
            first = jnp.logical_not(inside(z - step))

            @pl.when(inside(block) & first)
            def _(way=way, block=block):
                sum_copy(way, c, hop, partial.at[c, clamp(block)]).start()

            if hop > 1:
                @pl.when(inside(block) & jnp.logical_not(first))
                def _(way=way, block=block):
                    slot = arrived.at[way, c, hop - 2]
                    sum_copy(way, c, hop - 1, slot).wait_recv()
                    slot[...] = (slot[...].astype(F32) + partial[c, clamp(block)].astype(F32)).astype(BF16)
                    sum_copy(way, c, hop, slot).start()

    own_counts = counts_ref[pl.ds(me, 1), :].astype(F32)
    home_len = rows_all - jnp.sum(own_counts, axis=1, keepdims=True)

    def sum_finish(c):
        acc[...] = partial[c, z].astype(F32)
        for way in (0, 1):
            step = 1 - 2 * way

            @pl.when(inside(z - step))
            def _(way=way):
                slot = arrived.at[way, c, parts - 2]
                sum_copy(way, c, parts - 1, slot).wait_recv()
                acc[...] += slot[...].astype(F32)
        total = acc[...]
        final[rows_of(c), :] = total.astype(BF16)
        position = (lax.broadcasted_iota(jnp.int32, (count, 1), 0) + c * count).astype(F32)
        out_ref[rows_of(c), :] = jnp.where(position < home_len, total, 0.0).astype(BF16)

    def project(c):
        @pl.loop(0, wqkv.shape[1] // TILE)
        def _(i):
            columns = pl.ds(pl.multiple_of(i * TILE, TILE), TILE)
            total = jnp.zeros((count, TILE), F32)
            for b in range(parts):
                total += jnp.dot(
                    hid[b, rows_of(c), :],
                    wqkv[pl.ds(b * width, width), columns],
                    preferred_element_type=F32,
                )
            rounded = total.astype(BF16)
            for k in range(TILE // HD):
                heads[i * (TILE // HD) + k, rows_of(c), :] = rounded[:, k * HD:(k + 1) * HD]

    doc_row = docs_ref[...].astype(F32)

    def attend(c):
        seen = (c + 1) * count
        seen_rows = pl.ds(0, seen)
        query_at = lax.broadcasted_iota(jnp.int32, (count, seen), 0) + c * count
        key_at = lax.broadcasted_iota(jnp.int32, (count, seen), 1)
        same = doc_col[rows_of(c), :][:, :1] == doc_row[:, :seen]
        allowed = same & (key_at <= query_at)

        @pl.loop(0, kv_heads)
        def _(g):
            keys = heads[q_heads + g, seen_rows, :]
            values = heads[q_heads + kv_heads + g, seen_rows, :]
            for k in range(group):
                query = heads[g * group + k, rows_of(c), :]
                scores = lax.dot_general(
                    query, keys, (((1,), (1,)), ((), ())), preferred_element_type=F32
                ) * HD ** (-0.5)
                scores = jnp.where(allowed, scores, -jnp.inf)
                expo = jnp.exp(scores - jnp.max(scores, axis=1, keepdims=True))
                total = jnp.sum(expo, axis=1, keepdims=True)
                mix = jnp.dot(expo.astype(BF16), values, preferred_element_type=F32) / total
                columns = pl.ds(pl.multiple_of((g * group + k) * HD, HD), HD)
                mixed[:, columns] = mix.astype(BF16)

    def project_out(c):
        @pl.loop(0, parts * tiles_per_block)
        def _(i):
            columns = pl.ds(pl.multiple_of(i * TILE, TILE), TILE)
            total = jnp.dot(mixed[...], wout[:, columns], preferred_element_type=F32)
            inner = pl.ds(pl.multiple_of(lax.rem(i, tiles_per_block) * TILE, TILE), TILE)
            partial[c, lax.div(i, tiles_per_block), :, inner] = total.astype(BF16)

    gather_start(0, 1)
    for k in range(rows_all // HD):
        doc_col[pl.ds(k * HD, HD), :] = jnp.broadcast_to(doc_row[:, k * HD:(k + 1) * HD], (HD, HD)).T
    for hop in range(1, parts - 1):
        gather_take(0, hop)
    if chunks > 1:
        gather_start(1, 1)
    load_own.wait()
    for c in range(chunks):
        gather_take(c, parts - 1)
        if c == 0:
            for load in loads_qkv:
                load.wait()
        project(c)
        if c + 1 < chunks:
            for hop in range(1, parts - 2):
                gather_take(c + 1, hop)
        if c > 0:
            for hop in range(2, parts - 1):
                sum_hop(c - 1, hop)
        attend(c)
        if c == 0:
            load_out.wait()
        project_out(c)
        if c + 1 < chunks:
            gather_take(c + 1, parts - 2)
            if c + 2 < chunks:
                gather_start(c + 2, 1)
        if c > 0:
            sum_hop(c - 1, parts - 1)
        sum_hop(c, 1)
        if c > 0:
            sum_finish(c - 1)
    for hop in range(2, parts):
        sum_hop(chunks - 1, hop)
    sum_finish(chunks - 1)

    moved = peers * SLOT
    at = lax.broadcasted_iota(jnp.int32, (moved, peers), 0)
    to = lax.broadcasted_iota(jnp.int32, (moved, peers), 1)
    goal = lax.div(at, SLOT)
    counts = jnp.broadcast_to(own_counts, (moved, peers))
    length = jnp.sum(jnp.where(to == goal, counts, 0.0), axis=1, keepdims=True)
    before = jnp.sum(jnp.where(to < goal, counts, 0.0), axis=1, keepdims=True)
    place = lax.rem(lax.broadcasted_iota(jnp.int32, (moved, 1), 0), SLOT).astype(F32)
    index = jnp.where(place < length, home_len + before + place, -1.0)
    lanes = lax.broadcasted_iota(jnp.int32, (moved, rows_all), 1).astype(F32)
    pick = jnp.where(index == lanes, 1.0, 0.0).astype(BF16)
    outgoing[...] = jnp.dot(pick, final[...], preferred_element_type=F32).astype(BF16)

    def move_copy(i, goal, place):
        return pltpu.make_async_remote_copy(
            src_ref=outgoing.at[pl.ds(pl.multiple_of(goal * SLOT, SLOT), SLOT), :],
            dst_ref=slots.at[pl.ds(pl.multiple_of(place * SLOT, SLOT), SLOT), :],
            send_sem=mv_send.at[i - 1],
            recv_sem=mv_recv.at[i - 1],
            device_id={"dp": goal},
            device_id_type=MESH,
        )

    @pl.loop(1, peers)
    def _(i):
        move_copy(i, lax.rem(me + i, peers), me).start()

    slots[pl.ds(pl.multiple_of(me * SLOT, SLOT), SLOT), :] = outgoing[
        pl.ds(pl.multiple_of(me * SLOT, SLOT), SLOT), :
    ]

    for way in (0, 1):
        for hop in range(1, parts):
            @pl.when(gather_sends(way, hop))
            def _(way=way, hop=hop):
                for c in range(chunks):
                    gather_copy(way, c, hop).wait_send()

            @pl.when(inside(z + (1 - 2 * way) * (parts - hop)))
            def _(way=way, hop=hop):
                for c in range(chunks):
                    sum_copy(way, c, hop, arrived.at[way, c, hop - 1]).wait_send()

    @pl.loop(1, peers)
    def _(i):
        move_copy(i, lax.rem(me + i, peers), lax.rem(me + peers - i, peers)).wait()

    out_ref[pl.ds(rows_all, moved), :] = slots[...]


def on_device(hidden, w_query, w_key, w_value, w_out, doc_ids, send_counts):
    peers = lax.axis_size("dp")
    parts = lax.axis_size("tensor")
    rows, width = hidden.shape
    q_heads = w_query.shape[1] // HD
    kv_heads = w_key.shape[1] // HD
    chunks = CHUNKS
    count = rows // chunks
    features = w_query.shape[0]
    moved = peers * SLOT
    anywhere = pl.BlockSpec(memory_space=pl.ANY)
    in_vmem = pl.BlockSpec(memory_space=pltpu.VMEM)
    hops = parts - 1
    return pl.pallas_call(
        functools.partial(layer_kernel, peers, parts, chunks, q_heads, kv_heads),
        out_shape=jax.ShapeDtypeStruct((rows + moved, width), BF16),
        in_specs=[anywhere] * 5 + [in_vmem] * 2,
        out_specs=in_vmem,
        scratch_shapes=[
            pltpu.VMEM((features, (q_heads + 2 * kv_heads) * HD), BF16),
            pltpu.VMEM(w_out.shape, BF16),
            pltpu.VMEM((parts, rows, width), BF16),
            pltpu.VMEM((q_heads + 2 * kv_heads, rows, HD), BF16),
            pltpu.VMEM((count, q_heads * HD), BF16),
            pltpu.VMEM((chunks, parts, count, width), BF16),
            pltpu.VMEM((2, chunks, hops, count, width), BF16),
            pltpu.VMEM((count, width), F32),
            pltpu.VMEM((rows, width), BF16),
            pltpu.VMEM((moved, width), BF16),
            pltpu.VMEM((moved, width), BF16),
            pltpu.VMEM((rows, HD), F32),
            pltpu.SemaphoreType.DMA((5,)),
            pltpu.SemaphoreType.DMA((2, chunks, hops)),
            pltpu.SemaphoreType.DMA((2, chunks, hops)),
            pltpu.SemaphoreType.DMA((2, chunks, hops)),
            pltpu.SemaphoreType.DMA((2, chunks, hops)),
            pltpu.SemaphoreType.DMA((peers - 1,)),
            pltpu.SemaphoreType.DMA((peers - 1,)),
        ],
        compiler_params=pltpu.CompilerParams(
            collective_id=0, has_side_effects=True, vmem_limit_bytes=58 * 1024 * 1024
        ),
        name="layer",
    )(hidden, w_query, w_key, w_value, w_out, doc_ids.reshape(1, rows), send_counts)


def solution(mesh):
    in_specs = (
        P("dp", "tensor"),
        P(None, "tensor"),
        P(None, "tensor"),
        P(None, "tensor"),
        P("tensor", None),
        P("dp"),
        P(),
    )
    return jax.shard_map(
        on_device, mesh=mesh, in_specs=in_specs, out_specs=P("dp", "tensor"), check_vma=False
    )
```

```python
import functools

import jax
import jax.numpy as jnp
from jax import lax
from jax.experimental import pallas as pl
from jax.experimental.pallas import tpu as pltpu
from jax.sharding import PartitionSpec as P

HD = 128
SLOT = 16
TILE = 256
MESH = pl.DeviceIdType.MESH
F32 = jnp.float32
BF16 = jnp.bfloat16
SIZES = (64, 64, 128, 128, 64, 64)
ORDER = (
    ("send", 0), ("send", 1), ("take", 0, 1, 0), ("take", 0, 1, 1), ("send", 2), ("take", 0, 2, 0),
    ("take", 0, 3, 0), ("take", 0, 2, 1), ("take", 0, 3, 1), ("project", 0, 0), ("project", 0, 1),
    ("take", 1, 1, 0), ("attend", 0), ("take", 1, 1, 1), ("take", 1, 2, 1), ("out", 0, 0), ("out", 0, 1),
    ("take", 1, 2, 0), ("take", 1, 3, 0), ("send", 3), ("sum", 0, 1, 0), ("sum", 0, 1, 1), ("take", 1, 3, 1),
    ("project", 1, 0), ("project", 1, 1), ("attend", 1), ("out", 1, 0), ("out", 1, 1), ("take", 2, 1, 1),
    ("sum", 1, 1, 1), ("sum", 1, 1, 0), ("take", 2, 1, 0), ("take", 2, 2, 1), ("take", 2, 2, 0), ("take", 3, 1, 0),
    ("sum", 0, 2, 1), ("take", 3, 1, 1), ("sum", 1, 2, 0), ("sum", 0, 2, 0), ("send", 5), ("take", 2, 3, 1),
    ("send", 4), ("sum", 1, 3, 0), ("take", 2, 3, 0), ("sum", 1, 2, 1), ("project", 2, 0), ("project", 2, 1),
    ("attend", 2), ("take", 3, 2, 1), ("take", 3, 2, 0), ("sum", 0, 3, 1), ("out", 2, 0), ("out", 2, 1),
    ("sum", 2, 1, 1), ("sum", 2, 2, 1), ("sum", 2, 1, 0), ("take", 4, 1, 0), ("take", 5, 1, 0), ("take", 4, 1, 1),
    ("take", 5, 1, 1), ("sum", 2, 2, 0), ("sum", 2, 3, 1), ("take", 3, 3, 1), ("sum", 2, 3, 0), ("take", 3, 3, 0),
    ("project", 3, 0), ("project", 3, 1), ("take", 4, 2, 0), ("take", 4, 2, 1), ("sum", 0, 3, 0), ("sum", 1, 3, 1),
    ("attend", 3), ("out", 3, 0), ("out", 3, 1), ("sum", 3, 1, 1), ("take", 5, 2, 0), ("sum", 3, 2, 1),
    ("sum", 3, 1, 0), ("take", 4, 3, 0), ("sum", 3, 2, 0), ("take", 5, 2, 1), ("take", 4, 3, 1), ("project", 4, 0),
    ("project", 4, 1), ("attend", 4), ("out", 4, 0), ("out", 4, 1), ("sum", 3, 3, 0), ("sum", 4, 1, 1),
    ("take", 5, 3, 0), ("take", 5, 3, 1), ("sum", 3, 3, 1), ("project", 5, 0), ("project", 5, 1), ("attend", 5),
    ("sum", 4, 1, 0), ("out", 5, 0), ("out", 5, 1), ("sum", 5, 1, 0), ("finish", 0), ("sum", 4, 2, 0),
    ("sum", 5, 1, 1), ("sum", 4, 2, 1), ("sum", 5, 2, 0), ("sum", 5, 2, 1), ("finish", 2), ("sum", 4, 3, 1),
    ("finish", 1), ("sum", 4, 3, 0), ("sum", 5, 3, 1), ("sum", 5, 3, 0), ("finish", 4), ("finish", 3),
    ("finish", 5),
)


def plain_order(parts, chunks):
    last = parts - 1
    order = [("send", 0)]

    def both(kind, c, hops):
        for hop in hops:
            for way in (0, 1):
                order.append((kind, c, hop, way))

    both("take", 0, range(1, last))
    if chunks > 1:
        order.append(("send", 1))
    for c in range(chunks):
        both("take", c, (last,))
        order.extend([("project", c, 0), ("project", c, 1)])
        if c + 1 < chunks:
            both("take", c + 1, range(1, last - 1))
        if c > 0:
            both("sum", c - 1, range(2, last))
        order.extend([("attend", c), ("out", c, 0), ("out", c, 1)])
        if c + 1 < chunks:
            both("take", c + 1, (last - 1,))
            if c + 2 < chunks:
                order.append(("send", c + 2))
        if c > 0:
            both("sum", c - 1, (last,))
        both("sum", c, (1,))
        if c > 0:
            order.append(("finish", c - 1))
    both("sum", chunks - 1, range(2, parts))
    order.append(("finish", chunks - 1))
    return order


def layer_kernel(
    peers, parts, sizes, order, q_heads, kv_heads,
    hidden_ref, wq_ref, wk_ref, wv_ref, wo_ref, docs_ref, counts_ref,
    out_ref,
    wqkv, wout, hid, heads, mixed, partial, arrived, acc, final, outgoing, slots, doc_col,
    load_sem, ag_send, ag_recv, rs_send, rs_recv, mv_send, mv_recv,
):
    rows_all, width = hidden_ref.shape
    chunks = len(sizes)
    starts = [sum(sizes[:c]) for c in range(chunks)]
    group = q_heads // kv_heads
    me = lax.axis_index("dp")
    z = lax.axis_index("tensor")
    tiles_per_block = width // TILE

    def inside(position):
        return (position >= 0) & (position < parts)

    def clamp(position):
        return jnp.minimum(jnp.maximum(position, 0), parts - 1)

    q_cols, kv_cols = q_heads * HD, kv_heads * HD
    load_own = pltpu.make_async_copy(hidden_ref, hid.at[z], load_sem.at[0])
    loads_qkv = [
        pltpu.make_async_copy(wq_ref, wqkv.at[:, pl.ds(0, q_cols)], load_sem.at[1]),
        pltpu.make_async_copy(wk_ref, wqkv.at[:, pl.ds(q_cols, kv_cols)], load_sem.at[2]),
        pltpu.make_async_copy(wv_ref, wqkv.at[:, pl.ds(q_cols + kv_cols, kv_cols)], load_sem.at[3]),
    ]
    load_out = pltpu.make_async_copy(wo_ref, wout, load_sem.at[4])

    barrier = pltpu.get_barrier_semaphore()
    for step in (-1, 1):
        @pl.when(inside(z + step))
        def _(step=step):
            pl.semaphore_signal(barrier, inc=1, device_id={"tensor": z + step}, device_id_type=MESH)

    @pl.loop(1, peers)
    def _(i):
        pl.semaphore_signal(barrier, inc=1, device_id={"dp": lax.rem(me + i, peers)}, device_id_type=MESH)

    load_own.start()
    for load in loads_qkv:
        load.start()
    load_out.start()
    neighbours = inside(z - 1).astype(jnp.int32) + inside(z + 1).astype(jnp.int32)
    pl.semaphore_wait(barrier, peers - 1 + neighbours)

    def rows_of(c):
        return pl.ds(starts[c], sizes[c])

    def gather_copy(way, c, hop):
        step = 1 - 2 * way
        owner = clamp(z - step * (hop - 1))
        block = hid.at[owner, rows_of(c), :]
        return pltpu.make_async_remote_copy(
            src_ref=hidden_ref.at[rows_of(c), :] if hop == 1 else block,
            dst_ref=block,
            send_sem=ag_send.at[way, c, hop - 1],
            recv_sem=ag_recv.at[way, c, hop - 1],
            device_id={"tensor": clamp(z + step)},
            device_id_type=MESH,
        )

    def gather_sends(way, hop):
        step = 1 - 2 * way
        return inside(z - step * (hop - 1)) & inside(z + step)

    def gather_start(c):
        for way in (0, 1):
            @pl.when(gather_sends(way, 1))
            def _(way=way):
                gather_copy(way, c, 1).start()

    def gather_take(c, hop, way):
        step = 1 - 2 * way

        @pl.when(inside(z - step * hop))
        def _():
            block = hid.at[clamp(z - step * hop), rows_of(c), :]
            pltpu.make_async_remote_copy(
                src_ref=block,
                dst_ref=block,
                send_sem=ag_send.at[way, c, hop - 1],
                recv_sem=ag_recv.at[way, c, hop - 1],
                device_id={"tensor": clamp(z + step)},
                device_id_type=MESH,
            ).wait_recv()
            if hop < parts - 1:
                @pl.when(inside(z + step))
                def _():
                    gather_copy(way, c, hop + 1).start()

    def sum_copy(way, c, hop, source):
        step = 1 - 2 * way
        return pltpu.make_async_remote_copy(
            src_ref=source,
            dst_ref=arrived.at[way, hop - 1, rows_of(c), :],
            send_sem=rs_send.at[way, c, hop - 1],
            recv_sem=rs_recv.at[way, c, hop - 1],
            device_id={"tensor": clamp(z + step)},
            device_id_type=MESH,
        )

    def sum_hop(c, hop, way):
        step = 1 - 2 * way
        block = z + step * (parts - hop)
        first = jnp.logical_not(inside(z - step))
        own = partial.at[clamp(block), rows_of(c), :]

        @pl.when(inside(block) & first)
        def _():
            sum_copy(way, c, hop, own).start()

        if hop > 1:
            @pl.when(inside(block) & jnp.logical_not(first))
            def _():
                slot = arrived.at[way, hop - 2, rows_of(c), :]
                sum_copy(way, c, hop - 1, slot).wait_recv()
                slot[...] = (slot[...].astype(F32) + own[...].astype(F32)).astype(BF16)
                sum_copy(way, c, hop, slot).start()

    own_counts = counts_ref[pl.ds(me, 1), :].astype(F32)
    home_len = rows_all - jnp.sum(own_counts, axis=1, keepdims=True)

    def sum_finish(c):
        count = sizes[c]
        sums = acc.at[pl.ds(0, count), :]
        sums[...] = partial[z, rows_of(c), :].astype(F32)
        for way in (0, 1):
            step = 1 - 2 * way

            @pl.when(inside(z - step))
            def _(way=way):
                slot = arrived.at[way, parts - 2, rows_of(c), :]
                sum_copy(way, c, parts - 1, slot).wait_recv()
                sums[...] += slot[...].astype(F32)
        total = sums[...]
        final[rows_of(c), :] = total.astype(BF16)
        position = (lax.broadcasted_iota(jnp.int32, (count, 1), 0) + starts[c]).astype(F32)
        out_ref[rows_of(c), :] = jnp.where(position < home_len, total, 0.0).astype(BF16)

    def halves(total, half):
        middle = total // 2
        return (0, middle) if half == 0 else (middle, total)

    def project(c, half):
        count = sizes[c]

        @pl.loop(*halves(wqkv.shape[1] // TILE, half))
        def _(i):
            columns = pl.ds(pl.multiple_of(i * TILE, TILE), TILE)
            total = jnp.zeros((count, TILE), F32)
            for b in range(parts):
                total += jnp.dot(
                    hid[b, rows_of(c), :],
                    wqkv[pl.ds(b * width, width), columns],
                    preferred_element_type=F32,
                )
            rounded = total.astype(BF16)
            for k in range(TILE // HD):
                heads[i * (TILE // HD) + k, rows_of(c), :] = rounded[:, k * HD:(k + 1) * HD]

    doc_row = docs_ref[...].astype(F32)

    def attend(c):
        count = sizes[c]
        seen = starts[c] + count
        seen_rows = pl.ds(0, seen)
        query_at = lax.broadcasted_iota(jnp.int32, (count, seen), 0) + starts[c]
        key_at = lax.broadcasted_iota(jnp.int32, (count, seen), 1)
        same = doc_col[rows_of(c), :][:, :1] == doc_row[:, :seen]
        allowed = same & (key_at <= query_at)

        @pl.loop(0, kv_heads)
        def _(g):
            keys = heads[q_heads + g, seen_rows, :]
            values = heads[q_heads + kv_heads + g, seen_rows, :]
            for k in range(group):
                query = heads[g * group + k, rows_of(c), :]
                scores = lax.dot_general(
                    query, keys, (((1,), (1,)), ((), ())), preferred_element_type=F32
                ) * HD ** (-0.5)
                scores = jnp.where(allowed, scores, -jnp.inf)
                expo = jnp.exp(scores - jnp.max(scores, axis=1, keepdims=True))
                total = jnp.sum(expo, axis=1, keepdims=True)
                mix = jnp.dot(expo.astype(BF16), values, preferred_element_type=F32) / total
                columns = pl.ds(pl.multiple_of((g * group + k) * HD, HD), HD)
                mixed[pl.ds(0, count), columns] = mix.astype(BF16)

    def project_out(c, half):
        @pl.loop(*halves(parts * tiles_per_block, half))
        def _(i):
            columns = pl.ds(pl.multiple_of(i * TILE, TILE), TILE)
            total = jnp.dot(mixed[pl.ds(0, sizes[c]), :], wout[:, columns], preferred_element_type=F32)
            inner = pl.ds(pl.multiple_of(lax.rem(i, tiles_per_block) * TILE, TILE), TILE)
            partial[lax.div(i, tiles_per_block), rows_of(c), inner] = total.astype(BF16)

    for k in range(rows_all // HD):
        doc_col[pl.ds(k * HD, HD), :] = jnp.broadcast_to(doc_row[:, k * HD:(k + 1) * HD], (HD, HD)).T
    for step in order:
        kind, c = step[0], step[1]
        if kind == "send":
            gather_start(c)
        elif kind == "take":
            gather_take(c, step[2], step[3])
        elif kind == "project":
            if c == 0 and step[2] == 0:
                load_own.wait()
                for load in loads_qkv:
                    load.wait()
            project(c, step[2])
        elif kind == "attend":
            attend(c)
        elif kind == "out":
            if c == 0 and step[2] == 0:
                load_out.wait()
            project_out(c, step[2])
        elif kind == "sum":
            sum_hop(c, step[2], step[3])
        else:
            sum_finish(c)

    moved = peers * SLOT
    at = lax.broadcasted_iota(jnp.int32, (moved, peers), 0)
    to = lax.broadcasted_iota(jnp.int32, (moved, peers), 1)
    goal = lax.div(at, SLOT)
    counts = jnp.broadcast_to(own_counts, (moved, peers))
    length = jnp.sum(jnp.where(to == goal, counts, 0.0), axis=1, keepdims=True)
    before = jnp.sum(jnp.where(to < goal, counts, 0.0), axis=1, keepdims=True)
    place = lax.rem(lax.broadcasted_iota(jnp.int32, (moved, 1), 0), SLOT).astype(F32)
    index = jnp.where(place < length, home_len + before + place, -1.0)
    lanes = lax.broadcasted_iota(jnp.int32, (moved, rows_all), 1).astype(F32)
    pick = jnp.where(index == lanes, 1.0, 0.0).astype(BF16)
    outgoing[...] = jnp.dot(pick, final[...], preferred_element_type=F32).astype(BF16)

    def move_copy(i, goal, place):
        return pltpu.make_async_remote_copy(
            src_ref=outgoing.at[pl.ds(pl.multiple_of(goal * SLOT, SLOT), SLOT), :],
            dst_ref=slots.at[pl.ds(pl.multiple_of(place * SLOT, SLOT), SLOT), :],
            send_sem=mv_send.at[i - 1],
            recv_sem=mv_recv.at[i - 1],
            device_id={"dp": goal},
            device_id_type=MESH,
        )

    @pl.loop(1, peers)
    def _(i):
        move_copy(i, lax.rem(me + i, peers), me).start()

    slots[pl.ds(pl.multiple_of(me * SLOT, SLOT), SLOT), :] = outgoing[
        pl.ds(pl.multiple_of(me * SLOT, SLOT), SLOT), :
    ]

    for way in (0, 1):
        for hop in range(1, parts):
            @pl.when(gather_sends(way, hop))
            def _(way=way, hop=hop):
                for c in range(chunks):
                    gather_copy(way, c, hop).wait_send()

            @pl.when(inside(z + (1 - 2 * way) * (parts - hop)))
            def _(way=way, hop=hop):
                for c in range(chunks):
                    sum_copy(way, c, hop, arrived.at[way, hop - 1, rows_of(c), :]).wait_send()

    @pl.loop(1, peers)
    def _(i):
        move_copy(i, lax.rem(me + i, peers), lax.rem(me + peers - i, peers)).wait()

    out_ref[pl.ds(rows_all, moved), :] = slots[...]


def on_device(hidden, w_query, w_key, w_value, w_out, doc_ids, send_counts):
    peers = lax.axis_size("dp")
    parts = lax.axis_size("tensor")
    rows, width = hidden.shape
    q_heads = w_query.shape[1] // HD
    kv_heads = w_key.shape[1] // HD
    sizes = SIZES
    order = ORDER if parts == 4 else plain_order(parts, len(sizes))
    chunks, most = len(sizes), max(sizes)
    features = w_query.shape[0]
    moved = peers * SLOT
    anywhere = pl.BlockSpec(memory_space=pl.ANY)
    in_vmem = pl.BlockSpec(memory_space=pltpu.VMEM)
    hops = parts - 1
    return pl.pallas_call(
        functools.partial(layer_kernel, peers, parts, sizes, order, q_heads, kv_heads),
        out_shape=jax.ShapeDtypeStruct((rows + moved, width), BF16),
        in_specs=[anywhere] * 5 + [in_vmem] * 2,
        out_specs=in_vmem,
        scratch_shapes=[
            pltpu.VMEM((features, (q_heads + 2 * kv_heads) * HD), BF16),
            pltpu.VMEM(w_out.shape, BF16),
            pltpu.VMEM((parts, rows, width), BF16),
            pltpu.VMEM((q_heads + 2 * kv_heads, rows, HD), BF16),
            pltpu.VMEM((most, q_heads * HD), BF16),
            pltpu.VMEM((parts, rows, width), BF16),
            pltpu.VMEM((2, hops, rows, width), BF16),
            pltpu.VMEM((most, width), F32),
            pltpu.VMEM((rows, width), BF16),
            pltpu.VMEM((moved, width), BF16),
            pltpu.VMEM((moved, width), BF16),
            pltpu.VMEM((rows, HD), F32),
            pltpu.SemaphoreType.DMA((5,)),
            pltpu.SemaphoreType.DMA((2, chunks, hops)),
            pltpu.SemaphoreType.DMA((2, chunks, hops)),
            pltpu.SemaphoreType.DMA((2, chunks, hops)),
            pltpu.SemaphoreType.DMA((2, chunks, hops)),
            pltpu.SemaphoreType.DMA((peers - 1,)),
            pltpu.SemaphoreType.DMA((peers - 1,)),
        ],
        compiler_params=pltpu.CompilerParams(
            collective_id=0, has_side_effects=True, vmem_limit_bytes=58 * 1024 * 1024
        ),
        name="layer",
    )(hidden, w_query, w_key, w_value, w_out, doc_ids.reshape(1, rows), send_counts)


def solution(mesh):
    in_specs = (
        P("dp", "tensor"),
        P(None, "tensor"),
        P(None, "tensor"),
        P(None, "tensor"),
        P("tensor", None),
        P("dp"),
        P(),
    )
    return jax.shard_map(
        on_device, mesh=mesh, in_specs=in_specs, out_specs=P("dp", "tensor"), check_vma=False
    )
```
